512 devices in a mesh: tile: 128 (over y_lo, x, z), dir: 4 (over y_hi, core).
Axes of the slice: x: 4, y: 4 (y_hi: 2, y_lo: 2; y = y_hi * 2 + y_lo), z: 16, core: 2. Of those that a mesh axis runs over, the one named last changes fastest.
Arguments:
- layers: bfloat16 [4, 16384, 2048], P('dir', 'tile'), may hold values from -6 to 6
- offsets: int32 [4, 4, 2], replicated, may hold values from 0 to 8191, as said below
- subap_valid: int32 [128, 16], P('tile'), may hold values from 0 to 1, as said below
- defocus: float32 [3], replicated, may hold values from -0.08 to 0.08
- weights: float32 [3], replicated, may hold values from 0.25 to 1
Outputs:
- spots: bfloat16 [4, 128, 128, 2048], P('dir', 'tile')
The draws below stay inside these ranges and needn't reach their ends.
Inputs may be any that keep to these rules, and one draw needn't show every extreme that they name: offsets[d, l, 0] < 1024 and offsets[d, l, 1] < 8192; both bounds minus one are taken by some pair in every draw. `subap_valid`: the part of an annulus of lit subapertures that falls in the strip, with a few dead ones.
All inputs are finite; a program needn't handle non-finite values.
Results may differ from the reference program's by a relative error of at most 0.0055.
Values may be sent and summed in bfloat16 or wider, within the bound.
No kernel may reach another device: no remote copies, remote signals or barrier semaphores. Data moves between devices by JAX's collectives and lax.ppermute only.
A program may use at most 64 MiB of HBM per device.

```python
import math
import jax
import jax.numpy as jnp
from jax import lax

SUBPIX = 128
SPOT = 128
SUBX = 16
SLICES = 3
REACH = 2
QUANT = 4
OVER = 2
ROWS = 128
PCOLS = 2048
DIRS = 4
LAYERS = 4


def draw_offsets(key, part):
    keys = jax.random.split(jax.random.fold_in(key, 11), 3)
    row_bound = REACH * SUBPIX * QUANT
    col_bound = PCOLS * QUANT
    row_values = jax.random.randint(keys[0], (DIRS * LAYERS,), 0, row_bound, dtype=jnp.int32)
    col_values = jax.random.randint(keys[1], (DIRS * LAYERS,), 0, col_bound, dtype=jnp.int32)
    chosen = jax.random.permutation(keys[2], DIRS * LAYERS)
    row_values = row_values.at[chosen[0]].set(row_bound - 1).at[chosen[1]].set(0)
    col_values = col_values.at[chosen[2]].set(col_bound - 1)
    return jnp.stack([row_values, col_values], 1).reshape(DIRS, LAYERS, 2).astype(jnp.int32)


def draw_subap_valid(key, part):
    keys = jax.random.split(jax.random.fold_in(key, 23), 5)
    centre_row = jax.random.randint(keys[0], (), -4, 5, dtype=jnp.int32)
    outer_share = jax.random.randint(keys[2], (), 30, 71, dtype=jnp.int32)
    inner_most = (2 * SUBX - 1) * (2 * SUBX - 1) // 2 + 1
    inner = jax.random.randint(keys[3], (), 1, inner_most + 1, dtype=jnp.int32)
    row_twice = 2 * jnp.arange(ROWS, dtype=jnp.int32)[:, None] - (ROWS - 1) - centre_row
    col_twice = 2 * jnp.arange(SUBX, dtype=jnp.int32)[None, :] + 1
    radius = row_twice * row_twice + col_twice * col_twice
    outer = (ROWS + 4) * (ROWS + 4) + 4 * SUBX * SUBX * outer_share // 100
    alive = jax.random.randint(keys[4], (ROWS, SUBX), 0, 32, dtype=jnp.int32) != 0
    lit = (radius <= outer) & (radius >= inner) & alive
    return jnp.where(lit, 1, 0).astype(jnp.int32)


def level_of(own_key, dims, pieces, least, largest):
    def one(dim, blocks):
        heights = jax.random.uniform(jax.random.fold_in(jax.random.fold_in(own_key, 6), dim), (blocks,), jnp.float32, least / len(pieces), largest / len(pieces))
        return jnp.repeat(jnp.exp(heights), dims[dim] // blocks).reshape((-1,) + (1,) * (len(dims) - dim - 1))

    level = one(*pieces[0])
    for cut in pieces[1:]:
        level = level * one(*cut)
    return level


def noise(rng, extent, width, limit, shards=(), kind=jnp.bfloat16):
    array = width * jax.random.normal(rng, extent, jnp.float32)
    if shards:
        array = array * level_of(rng, extent, shards, -0.22, 0.18)
    return jnp.clip(array, -limit, limit).astype(kind)


def setup_inputs(seed: int = 0) -> dict:
    arg_keys = jax.random.split(jax.random.key(seed), 6)
    layers = noise(arg_keys[0], (LAYERS, ROWS * SUBPIX, PCOLS), 1.0, 6.0, ((0, 4), (1, 128)))
    offsets = draw_offsets(jax.random.fold_in(arg_keys[5], 71), 0)
    subap_valid = draw_subap_valid(jax.random.fold_in(arg_keys[5], 71), 0)
    defocus = jnp.clip(jax.random.uniform(arg_keys[3], (SLICES,), jnp.float32, -0.08, 0.08), -0.08, 0.08)
    weights = jnp.clip(jnp.exp(jax.random.uniform(arg_keys[4], (SLICES,), jnp.float32, math.log(0.25), math.log(1.0))), 0.25, 1.0)
    return dict(layers=layers, offsets=offsets, subap_valid=subap_valid, defocus=defocus, weights=weights)


def tables():
    frequency = jnp.arange(SPOT, dtype=jnp.float32) - SPOT // 2
    position = jnp.arange(SUBPIX, dtype=jnp.float32) - (SUBPIX - 1) / 2.0
    phase_angle = -2.0 * math.pi / (OVER * SUBPIX) * frequency[:, None] * position[None, :]
    factor = 1.0 / math.sqrt(SUBPIX)
    real_part = jnp.cos(phase_angle) * factor
    imag_part = jnp.sin(phase_angle) * factor
    left_table = jnp.concatenate([jnp.concatenate([real_part, -imag_part], 1), jnp.concatenate([imag_part, real_part], 1)], 0).astype(jnp.bfloat16)
    right_table = jnp.concatenate([jnp.concatenate([real_part.T, imag_part.T], 1), jnp.concatenate([-imag_part.T, real_part.T], 1)], 0).astype(jnp.bfloat16)
    return (left_table, right_table)

def interpolate(window, offset_pair):
    col_steps = offset_pair[1] // QUANT
    col_frac = (offset_pair[1] % QUANT).astype(jnp.float32) / QUANT
    row_frac = (offset_pair[0] % QUANT).astype(jnp.float32) / QUANT
    col_first = jnp.roll(window, -col_steps, axis=1)
    col_second = jnp.roll(window, -(col_steps + 1), axis=1)
    across = (1.0 - col_frac) * col_first + col_frac * col_second
    return ((1.0 - row_frac) * across[:-1] + row_frac * across[1:]).astype(jnp.bfloat16)

def spots_row(pupil_phase, first_row, total_rows, defocus, weights, valid_row):
    left_table, right_table = tables()
    row_position = ((first_row + jnp.arange(SUBPIX, dtype=jnp.int32)).astype(jnp.float32) - (total_rows - 1) / 2.0) / SUBPIX
    col_position = (jnp.arange(PCOLS, dtype=jnp.float32) - (PCOLS - 1) / 2.0) / SUBPIX
    radius = row_position[:, None] ** 2 + col_position[None, :] ** 2
    spot_sum = jnp.zeros((SPOT * SUBX, SPOT), jnp.float32)
    for altitude in range(SLICES):
        phase_angle = pupil_phase + defocus[altitude] * radius
        pupil_field = jnp.concatenate([jnp.cos(phase_angle), jnp.sin(phase_angle)], 0).astype(jnp.bfloat16)
        focal_plane = jnp.dot(left_table, pupil_field, preferred_element_type=jnp.float32).astype(jnp.bfloat16)
        blocks = jnp.concatenate([focal_plane[:SPOT].reshape(SPOT * SUBX, SUBPIX), focal_plane[SPOT:].reshape(SPOT * SUBX, SUBPIX)], 1)
        spot_field = jnp.dot(blocks, right_table, preferred_element_type=jnp.float32)
        spot_sum = spot_sum + weights[altitude] * (spot_field[:, :SPOT] ** 2 + spot_field[:, SPOT:] ** 2)
    scaled = spot_sum / jnp.sum(weights)
    masked = scaled.reshape(SPOT, SUBX, SPOT) * valid_row.astype(jnp.float32)[None, :, None]
    return masked.reshape(SPOT, SUBX * SPOT).astype(jnp.bfloat16)

def reference(layers, offsets, subap_valid, defocus, weights):
    total_rows = ROWS * SUBPIX

    def one_direction(direction):
        offset_pairs = offsets[direction]

        def one_row(row_index):
            pupil_phase = jnp.zeros((SUBPIX, PCOLS), jnp.float32)
            for layer_index in range(LAYERS):
                offset_pair = offset_pairs[layer_index]
                start_row = row_index * SUBPIX + offset_pair[0] // QUANT
                rows_index = ((start_row + jnp.arange(SUBPIX + 1, dtype=jnp.int32)) % total_rows).astype(jnp.int32)
                window = jnp.take(layers[layer_index], rows_index, axis=0).astype(jnp.float32)
                pupil_phase = pupil_phase + interpolate(window, offset_pair).astype(jnp.float32)
            return spots_row(pupil_phase, row_index * SUBPIX, total_rows, defocus, weights, subap_valid[row_index])
        return lax.map(one_row, jnp.arange(ROWS, dtype=jnp.int32))
    return lax.map(one_direction, jnp.arange(DIRS, dtype=jnp.int32))
```

```python
import functools
import math

import jax
import jax.numpy as jnp
import numpy as np
from jax import lax
from jax.experimental import pallas as pl
from jax.experimental.pallas import tpu as pltpu
from jax.sharding import PartitionSpec as P

SUBPIX = 128
SPOT = 128
SUBX = 16
SLICES = 3
QUANT = 4
OVER = 2
PCOLS = 2048
DIRS = 4

CUTS = (0, 64, 128)
FINAL_COLS = 512
VMEM_LIMIT = 48 * 1024 * 1024


def tables():
    frequency = np.arange(SPOT, dtype=np.float64) - SPOT // 2
    position = np.arange(SUBPIX, dtype=np.float64) - (SUBPIX - 1) / 2.0
    angle = -2.0 * math.pi / (OVER * SUBPIX) * frequency[:, None] * position[None, :]
    factor = 1.0 / math.sqrt(SUBPIX)
    real_part = (np.cos(angle) * factor).astype(jnp.bfloat16)
    imag_part = (np.sin(angle) * factor).astype(jnp.bfloat16)
    right = np.block([[real_part.T, imag_part.T], [-imag_part.T, real_part.T]])
    return real_part.astype(np.float32), imag_part.astype(np.float32), right


def shifted(value, by):
    count = lax.axis_size("tile")
    return lax.ppermute(value, "tile", [(i, (i + by) % count) for i in range(count)])


def other_core(value):
    return lax.ppermute(value, "dir", [(0, 1), (1, 0), (2, 3), (3, 2)])


def other_chip(value):
    return lax.ppermute(value, "dir", [(0, 2), (1, 3), (2, 0), (3, 1)])


def term_kernel(first, rows, depths, index_ref, offsets_ref, *refs):
    blocks = refs[: len(depths)]
    outs = refs[len(depths) :]
    total = sum(depths)
    own = index_ref[0]
    wanted = (own, own ^ 2, own ^ 1, own ^ 3)
    parts = []
    for direction in wanted:
        steps = offsets_ref[direction, own, 0]
        start = steps >> 2
        frac = (steps & 3).astype(jnp.float32) * 0.25
        away = lax.broadcasted_iota(jnp.int32, (rows, total), 1) - lax.broadcasted_iota(
            jnp.int32, (rows, total), 0
        )
        parts.append(
            jnp.where(away == start, 1.0 - frac, jnp.where(away == start + 1, frac, 0.0))
        )
    select = jnp.concatenate(parts, 0).astype(jnp.bfloat16)
    down = None
    at = 0
    for block, depth in zip(blocks, depths):
        piece = jnp.dot(
            select[:, at : at + depth], block[...], preferred_element_type=jnp.float32
        )
        down = piece if down is None else down + piece
        at += depth
    for place, direction in enumerate(wanted):
        steps = offsets_ref[direction, own, 1]
        start = steps >> 2
        frac = (steps & 3).astype(jnp.float32) * 0.25
        rows_down = down[place * rows : (place + 1) * rows]
        near = pltpu.roll(rows_down, (PCOLS - start) & (PCOLS - 1), 1)
        far = pltpu.roll(near, PCOLS - 1, 1)
        term = ((1.0 - frac) * near + frac * far).astype(jnp.bfloat16)
        if place < 2:
            outs[place][...] = term
        else:
            outs[2][place - 2] = term


def terms(first, rows, index, offsets, blocks):
    depths = tuple(b.shape[0] for b in blocks)
    flat = jax.ShapeDtypeStruct((rows, PCOLS), jnp.bfloat16)
    whole = pl.BlockSpec(memory_space=pltpu.VMEM)
    return pl.pallas_call(
        functools.partial(term_kernel, first, rows, depths),
        out_shape=(flat, flat, jax.ShapeDtypeStruct((2, rows, PCOLS), jnp.bfloat16)),
        in_specs=[pl.BlockSpec(memory_space=pltpu.SMEM)] * 2 + [whole] * len(blocks),
        out_specs=(whole, whole, whole),
        compiler_params=pltpu.CompilerParams(vmem_limit_bytes=VMEM_LIMIT),
        name="terms",
    )(index, offsets, *blocks)


def series():
    points = 0.25 * (1.0 - np.cos(np.pi * (np.arange(4000) + 0.5) / 4000)) * 0.5
    basis = lambda count: np.stack([points**k for k in range(count)], 1)
    root = np.sqrt(points)
    sine = np.linalg.lstsq(basis(8), np.sin(2 * np.pi * root) / root, rcond=None)[0]
    cosine = np.linalg.lstsq(basis(8), np.cos(2 * np.pi * root), rcond=None)[0]
    return [float(c) for c in sine], [float(c) for c in cosine]


SINE, COSINE = series()


def horner(coefficients, square):
    value = jnp.full_like(square, coefficients[-1])
    for c in coefficients[-2::-1]:
        value = value * square + c
    return value


def final_kernel(chunks, scale_ref, valid_ref, left_ref, right_ref, column_ref, *refs):
    keeps, pairs, fars = refs[:chunks], refs[chunks : 2 * chunks], refs[2 * chunks : 3 * chunks]
    out_ref = refs[3 * chunks]
    cols = out_ref.shape[1]
    phase = jnp.concatenate(
        [
            (k[...].astype(jnp.float32) + p[0].astype(jnp.float32)) + f[...].astype(jnp.float32)
            for k, p, f in zip(keeps, pairs, fars)
        ],
        0,
    )
    turns = phase * (0.5 / math.pi)
    turns = turns - jnp.round(turns)
    square = turns * turns
    field = jnp.concatenate(
        [horner(COSINE, square), turns * horner(SINE, square)], 0
    ).astype(jnp.bfloat16)
    focal = jnp.dot(left_ref[...], field, preferred_element_type=jnp.float32)
    reals, imags = [], []
    for altitude in range(SLICES):
        real = focal[2 * SPOT * altitude : 2 * SPOT * altitude + SPOT]
        imag = focal[2 * SPOT * altitude + SPOT : 2 * SPOT * (altitude + 1)]
        cosine = column_ref[altitude : altitude + 1]
        sine = column_ref[SLICES + altitude : SLICES + altitude + 1]
        reals.append((real * cosine - imag * sine).astype(jnp.bfloat16))
        imags.append((real * sine + imag * cosine).astype(jnp.bfloat16))
    real = jnp.concatenate(reals, 0)
    imag = jnp.concatenate(imags, 0)
    for place in range(cols // SUBPIX):
        at = slice(place * SUBPIX, (place + 1) * SUBPIX)
        spot = jnp.dot(
            jnp.concatenate([real[:, at], imag[:, at]], 1),
            right_ref[...],
            preferred_element_type=jnp.float32,
        )
        power = spot * spot
        power = power[:, :SPOT] + power[:, SPOT:]
        total = None
        for altitude in range(SLICES):
            piece = scale_ref[altitude] * power[altitude * SPOT : (altitude + 1) * SPOT]
            total = piece if total is None else total + piece
        lit = valid_ref[0, pl.program_id(0) * (cols // SUBPIX) + place].astype(jnp.float32)
        out_ref[:, at] = (total * lit).astype(jnp.bfloat16)


def spots_of(scale, valid, left, right, column, keeps, pairs, fars):
    chunks = len(keeps)
    smem = pl.BlockSpec(memory_space=pltpu.SMEM)
    flat = [pl.BlockSpec((k.shape[0], FINAL_COLS), lambda i: (0, i)) for k in keeps]
    deep = [pl.BlockSpec((1, k.shape[0], FINAL_COLS), lambda i: (0, 0, i)) for k in keeps]
    return pl.pallas_call(
        functools.partial(final_kernel, chunks),
        grid=(PCOLS // FINAL_COLS,),
        out_shape=jax.ShapeDtypeStruct((SPOT, PCOLS), jnp.bfloat16),
        in_specs=[
            smem,
            smem,
            pl.BlockSpec(left.shape, lambda i: (0, 0)),
            pl.BlockSpec(right.shape, lambda i: (0, 0)),
            pl.BlockSpec((2 * SLICES, FINAL_COLS), lambda i: (0, i)),
        ]
        + flat
        + deep
        + flat,
        out_specs=pl.BlockSpec((SPOT, FINAL_COLS), lambda i: (0, i)),
        compiler_params=pltpu.CompilerParams(vmem_limit_bytes=VMEM_LIMIT),
        name="spots",
    )(scale, valid, left, right, column, *keeps, *pairs, *fars)


def shards(layers, offsets, subap_valid, defocus, weights):
    index = lax.axis_index("dir").astype(jnp.int32)[None]
    tile = lax.axis_index("tile")
    total_rows = lax.axis_size("tile") * SUBPIX
    block = layers[0]
    own = [block[a:b] for a, b in zip(CUTS, CUTS[1:])]
    once = [shifted(piece, -1) for piece in own]
    twice = [shifted(piece, -1) for piece in once]

    real_part, imag_part, right = tables()
    row = (
        (tile * SUBPIX + jnp.arange(SUBPIX, dtype=jnp.int32)).astype(jnp.float32)
        - (total_rows - 1) / 2.0
    ) / SUBPIX
    col = (jnp.arange(PCOLS, dtype=jnp.float32) - (PCOLS - 1) / 2.0) / SUBPIX
    row_angle = defocus[:, None] * (row * row)[None, :]
    col_angle = defocus[:, None] * (col * col)[None, :]
    row_cos, row_sin = jnp.cos(row_angle)[:, None], jnp.sin(row_angle)[:, None]
    left_real = real_part[None] * row_cos - imag_part[None] * row_sin
    left_imag = real_part[None] * row_sin + imag_part[None] * row_cos
    left = jnp.concatenate(
        [
            jnp.concatenate([left_real, -left_imag], 2),
            jnp.concatenate([left_imag, left_real], 2),
        ],
        1,
    )
    left = left.reshape(SLICES * 2 * SPOT, 2 * SUBPIX).astype(jnp.bfloat16)
    column = jnp.concatenate([jnp.cos(col_angle), jnp.sin(col_angle)], 0)
    scale = weights / jnp.sum(weights)

    keeps, pairs, fars = [], [], []
    for m, (a, b) in enumerate(zip(CUTS, CUTS[1:])):
        blocks = own[m:] + once + twice[: m + 1]
        keep, send, cross = terms(a, b - a, index, offsets, blocks)
        pair = other_core(cross)
        both = (send.astype(jnp.float32) + pair[1].astype(jnp.float32)).astype(jnp.bfloat16)
        keeps.append(keep)
        pairs.append(pair)
        fars.append(other_chip(both))
    spots = spots_of(scale, subap_valid, left, right, column, keeps, pairs, fars)
    return spots[None, None]


def solution(mesh):
    placed = (P("dir", "tile", None), P(), P("tile", None), P(), P())
    return jax.shard_map(
        shards, mesh=mesh, in_specs=placed, out_specs=P("dir", "tile", None, None), check_vma=False
    )
```

```python
import functools
import math

import jax
import jax.numpy as jnp
import numpy as np
from jax import lax
from jax.experimental import pallas as pl
from jax.experimental.pallas import tpu as pltpu
from jax.sharding import PartitionSpec as P

SUBPIX = 128
SPOT = 128
SUBX = 16
SLICES = 3
QUANT = 4
OVER = 2
PCOLS = 2048
DIRS = 4

CUTS = (0, 64, 128)
FINAL_COLS = 512
LANES = 128
GROUP = 256
VMEM_LIMIT = 48 * 1024 * 1024


def tables():
    frequency = np.arange(SPOT, dtype=np.float64) - SPOT // 2
    position = np.arange(SUBPIX, dtype=np.float64) - (SUBPIX - 1) / 2.0
    angle = -2.0 * math.pi / (OVER * SUBPIX) * frequency[:, None] * position[None, :]
    factor = 1.0 / math.sqrt(SUBPIX)
    real_part = (np.cos(angle) * factor).astype(jnp.bfloat16)
    imag_part = (np.sin(angle) * factor).astype(jnp.bfloat16)
    right = np.block([[real_part.T, imag_part.T], [-imag_part.T, real_part.T]])
    return real_part.astype(np.float32), imag_part.astype(np.float32), right


def shifted(value, by):
    count = lax.axis_size("tile")
    return lax.ppermute(value, "tile", [(i, (i + by) % count) for i in range(count)])


def other_core(value):
    return lax.ppermute(value, "dir", [(0, 1), (1, 0), (2, 3), (3, 2)])


def other_chip(value):
    return lax.ppermute(value, "dir", [(0, 2), (1, 3), (2, 0), (3, 1)])


def term_kernel(first, rows, depths, index_ref, offsets_ref, *refs):
    blocks = refs[: len(depths)]
    outs = refs[len(depths) :]
    total = sum(depths)
    own = index_ref[0]
    wanted = (own, own ^ 2, own ^ 1, own ^ 3)
    parts = []
    for direction in wanted:
        steps = offsets_ref[direction, own, 0]
        start = steps >> 2
        frac = (steps & 3).astype(jnp.float32) * 0.25
        away = lax.broadcasted_iota(jnp.int32, (rows, total), 1) - lax.broadcasted_iota(
            jnp.int32, (rows, total), 0
        )
        parts.append(
            jnp.where(away == start, 1.0 - frac, jnp.where(away == start + 1, frac, 0.0))
        )
    select = jnp.concatenate(parts, 0).astype(jnp.bfloat16)
    lane = lax.broadcasted_iota(jnp.int32, (rows, LANES), 1)
    moves = []
    for place, direction in enumerate(wanted):
        steps = offsets_ref[direction, own, 1]
        start = steps >> 2
        frac = (steps & 3).astype(jnp.float32) * 0.25
        within = start & (LANES - 1)
        moves.append((start >> 7, within, (LANES - within) & (LANES - 1), frac))

    def columns(at):
        window = jnp.concatenate([block[:, at : at + GROUP] for block in blocks], 0)
        down = jnp.dot(select, window, preferred_element_type=jnp.float32)
        return [down[:, k : k + LANES] for k in range(0, GROUP, LANES)]

    wide = lax.broadcasted_iota(jnp.int32, (DIRS * rows, LANES), 1)

    def finish(place, k, here, after):
        skip, within = moves[place][:2]
        term = jnp.where(lane < LANES - within, here, after).astype(jnp.bfloat16)
        to = pl.ds(pl.multiple_of(((k - skip) & (PCOLS // LANES - 1)) * LANES, LANES), LANES)
        outs[place][:, to] = term

    def turned(value, ahead):
        out = []
        for place in range(DIRS):
            at = slice(place * rows, (place + 1) * rows)
            _, _, turn, frac = moves[place]
            out.append(pltpu.roll((1.0 - frac) * value[at] + frac * ahead[at], turn, 1))
        return out

    def shift(value):
        return pltpu.roll(value, LANES - 1, 1)

    count = PCOLS // LANES
    values, shifts, turns = {}, {}, {}

    def get(k):
        if k not in values:
            k -= k % (GROUP // LANES)
            for n, value in enumerate(columns(k * LANES)):
                values[k + n] = value
                shifts[k + n] = shift(value)

    get(0)
    for k in range(count):
        get((k + 1) % count)
        ahead = jnp.where(wide < LANES - 1, shifts[k], shifts[(k + 1) % count])
        turns[k] = turned(values[k], ahead)
        if k:
            for place in range(DIRS):
                finish(place, k - 1, turns[k - 1][place], turns[k][place])
    for place in range(DIRS):
        finish(place, count - 1, turns[count - 1][place], turns[0][place])


def terms(first, rows, index, offsets, blocks):
    depths = tuple(b.shape[0] for b in blocks)
    flat = jax.ShapeDtypeStruct((rows, PCOLS), jnp.bfloat16)
    whole = pl.BlockSpec(memory_space=pltpu.VMEM)
    return pl.pallas_call(
        functools.partial(term_kernel, first, rows, depths),
        out_shape=(flat,) * DIRS,
        in_specs=[pl.BlockSpec(memory_space=pltpu.SMEM)] * 2 + [whole] * len(blocks),
        out_specs=(whole,) * DIRS,
        compiler_params=pltpu.CompilerParams(vmem_limit_bytes=VMEM_LIMIT),
        cost_estimate=pl.CostEstimate(flops=1024, bytes_accessed=1024, transcendentals=0),
        name="terms",
    )(index, offsets, *blocks)


def series():
    points = 0.25 * (1.0 - np.cos(np.pi * (np.arange(4000) + 0.5) / 4000)) * 0.5
    basis = lambda count: np.stack([points**k for k in range(count)], 1)
    root = np.sqrt(points)
    sine = np.linalg.lstsq(basis(8), np.sin(2 * np.pi * root) / root, rcond=None)[0]
    cosine = np.linalg.lstsq(basis(8), np.cos(2 * np.pi * root), rcond=None)[0]
    return [float(c) for c in sine], [float(c) for c in cosine]


SINE, COSINE = series()


def horner(coefficients, square):
    value = jnp.full_like(square, coefficients[-1])
    for c in coefficients[-2::-1]:
        value = value * square + c
    return value


def final_kernel(chunks, left_ref, right_ref, column_ref, *refs):
    keeps, pairs, fars = refs[:chunks], refs[chunks : 2 * chunks], refs[2 * chunks : 3 * chunks]
    out_ref = refs[3 * chunks]
    cols = out_ref.shape[1]
    phase = jnp.concatenate(
        [
            (k[...].astype(jnp.float32) + p[...].astype(jnp.float32)) + f[...].astype(jnp.float32)
            for k, p, f in zip(keeps, pairs, fars)
        ],
        0,
    )
    turns = phase * (0.5 / math.pi)
    turns = turns - jnp.round(turns)
    square = turns * turns
    field = jnp.concatenate(
        [horner(COSINE, square), turns * horner(SINE, square)], 0
    ).astype(jnp.bfloat16)
    focal = jnp.dot(left_ref[...], field, preferred_element_type=jnp.float32)
    reals, imags = [], []
    for altitude in range(SLICES):
        real = focal[2 * SPOT * altitude : 2 * SPOT * altitude + SPOT]
        imag = focal[2 * SPOT * altitude + SPOT : 2 * SPOT * (altitude + 1)]
        cosine = column_ref[altitude : altitude + 1]
        sine = column_ref[SLICES + altitude : SLICES + altitude + 1]
        reals.append((real * cosine - imag * sine).astype(jnp.bfloat16))
        imags.append((real * sine + imag * cosine).astype(jnp.bfloat16))
    real = jnp.concatenate(reals, 0)
    imag = jnp.concatenate(imags, 0)
    for place in range(cols // SUBPIX):
        at = slice(place * SUBPIX, (place + 1) * SUBPIX)
        spot = jnp.dot(
            jnp.concatenate([real[:, at], imag[:, at]], 1),
            right_ref[...],
            preferred_element_type=jnp.float32,
        )
        power = spot * spot
        power = power[:, :SPOT] + power[:, SPOT:]
        total = None
        for altitude in range(SLICES):
            piece = power[altitude * SPOT : (altitude + 1) * SPOT]
            total = piece if total is None else total + piece
        lit = column_ref[2 * SLICES : 2 * SLICES + 1, at]
        out_ref[:, at] = (total * lit).astype(jnp.bfloat16)


def spots_of(left, right, column, keeps, pairs, fars):
    chunks = len(keeps)
    flat = [pl.BlockSpec((k.shape[0], FINAL_COLS), lambda i: (0, i)) for k in keeps]
    return pl.pallas_call(
        functools.partial(final_kernel, chunks),
        grid=(PCOLS // FINAL_COLS,),
        out_shape=jax.ShapeDtypeStruct((SPOT, PCOLS), jnp.bfloat16),
        in_specs=[
            pl.BlockSpec(left.shape, lambda i: (0, 0)),
            pl.BlockSpec(right.shape, lambda i: (0, 0)),
            pl.BlockSpec((2 * SLICES + 1, FINAL_COLS), lambda i: (0, i)),
        ]
        + flat * 3,
        out_specs=pl.BlockSpec((SPOT, FINAL_COLS), lambda i: (0, i)),
        compiler_params=pltpu.CompilerParams(vmem_limit_bytes=VMEM_LIMIT),
        name="spots",
    )(left, right, column, *keeps, *pairs, *fars)


def shards(layers, offsets, subap_valid, defocus, weights):
    index = lax.axis_index("dir").astype(jnp.int32)[None]
    tile = lax.axis_index("tile")
    total_rows = lax.axis_size("tile") * SUBPIX
    block = layers[0]
    own = [block[a:b] for a, b in zip(CUTS, CUTS[1:])]
    once = [shifted(piece, -1) for piece in own]

    real_part, imag_part, right = tables()
    row = (
        (tile * SUBPIX + jnp.arange(SUBPIX, dtype=jnp.int32)).astype(jnp.float32)
        - (total_rows - 1) / 2.0
    ) / SUBPIX
    col = (jnp.arange(PCOLS, dtype=jnp.float32) - (PCOLS - 1) / 2.0) / SUBPIX
    row_angle = defocus[:, None] * (row * row)[None, :]
    col_angle = defocus[:, None] * (col * col)[None, :]
    row_cos, row_sin = jnp.cos(row_angle)[:, None], jnp.sin(row_angle)[:, None]
    left_real = real_part[None] * row_cos - imag_part[None] * row_sin
    left_imag = real_part[None] * row_sin + imag_part[None] * row_cos
    left = jnp.concatenate(
        [
            jnp.concatenate([left_real, -left_imag], 2),
            jnp.concatenate([left_imag, left_real], 2),
        ],
        1,
    )
    left = left.reshape(SLICES * 2 * SPOT, 2 * SUBPIX).astype(jnp.bfloat16)
    share = jnp.sqrt(weights / jnp.sum(weights))[:, None]
    lit = jnp.repeat(subap_valid.astype(jnp.float32), SUBPIX, axis=1)
    column = jnp.concatenate([jnp.cos(col_angle) * share, jnp.sin(col_angle) * share, lit], 0)

    once[0], offsets, left, column = lax.optimization_barrier((once[0], offsets, left, column))
    twice = [shifted(piece, -1) for piece in once]

    blocks = own + once + twice[:1]
    keep, send, cross, cross_send = terms(0, CUTS[1], index, offsets, blocks)
    joined = other_core(cross_send)
    joined, twice[1] = lax.optimization_barrier((joined, twice[1]))
    both = (send.astype(jnp.float32) + joined.astype(jnp.float32)).astype(jnp.bfloat16)
    both, twice[1] = lax.optimization_barrier((both, twice[1]))
    keeps, crosses, fars = [keep], [cross], [other_chip(both)]

    blocks = own[1:] + once + twice
    keep, send, cross, cross_send = terms(CUTS[1], CUTS[2] - CUTS[1], index, offsets, blocks)
    joined = other_core(cross_send)
    send, fars[0] = lax.optimization_barrier((send, fars[0]))
    both = (send.astype(jnp.float32) + joined.astype(jnp.float32)).astype(jnp.bfloat16)
    crosses.append(cross)
    keeps.append(keep)
    fars.append(other_chip(both))
    crosses[0], crosses[1], both = lax.optimization_barrier((crosses[0], crosses[1], both))
    pairs = [other_core(cross) for cross in crosses]
    fars[1], column = lax.optimization_barrier((fars[1], column))
    spots = spots_of(left, right, column, keeps, pairs, fars)
    return spots[None, None]


def solution(mesh):
    placed = (P("dir", "tile", None), P(), P("tile", None), P(), P())
    return jax.shard_map(
        shards, mesh=mesh, in_specs=placed, out_specs=P("dir", "tile", None, None), check_vma=False
    )
```

```python
import functools
import math

import jax
import jax.numpy as jnp
import numpy as np
from jax import lax
from jax.experimental import pallas as pl
from jax.experimental.pallas import tpu as pltpu
from jax.sharding import PartitionSpec as P

SUBPIX = 128
SPOT = 128
SUBX = 16
SLICES = 3
QUANT = 4
OVER = 2
PCOLS = 2048
DIRS = 4

CUTS = (0, 64, 128)
SIDES = (0, 1024, 2048)
FINAL_COLS = 512
LANES = 128
GROUP = 256
VMEM_LIMIT = 48 * 1024 * 1024


def tables():
    frequency = np.arange(SPOT, dtype=np.float64) - SPOT // 2
    position = np.arange(SUBPIX, dtype=np.float64) - (SUBPIX - 1) / 2.0
    angle = -2.0 * math.pi / (OVER * SUBPIX) * frequency[:, None] * position[None, :]
    factor = 1.0 / math.sqrt(SUBPIX)
    real_part = (np.cos(angle) * factor).astype(jnp.bfloat16)
    imag_part = (np.sin(angle) * factor).astype(jnp.bfloat16)
    right = np.block([[real_part.T, imag_part.T], [-imag_part.T, real_part.T]])
    return real_part.astype(np.float32), imag_part.astype(np.float32), right


def shifted(value, by):
    count = lax.axis_size("tile")
    return lax.ppermute(value, "tile", [(i, (i + by) % count) for i in range(count)])


def other_core(value):
    return lax.ppermute(value, "dir", [(0, 1), (1, 0), (2, 3), (3, 2)])


def other_chip(value):
    return lax.ppermute(value, "dir", [(0, 2), (1, 3), (2, 0), (3, 1)])


def term_kernel(first, rows, depths, carried, index_ref, offsets_ref, *refs):
    blocks = refs[: len(depths)]
    outs = refs[len(depths) + carried :]
    if carried:
        outs[2][2] = refs[len(depths)][...]
        outs = (outs[0], outs[1], outs[2].at[1], outs[2].at[0])
    total = sum(depths)
    own = index_ref[0]
    wanted = (own, own ^ 2, own ^ 1, own ^ 3)
    parts = []
    for direction in wanted:
        steps = offsets_ref[direction, own, 0]
        start = steps >> 2
        frac = (steps & 3).astype(jnp.float32) * 0.25
        away = lax.broadcasted_iota(jnp.int32, (rows, total), 1) - lax.broadcasted_iota(
            jnp.int32, (rows, total), 0
        )
        parts.append(
            jnp.where(away == start, 1.0 - frac, jnp.where(away == start + 1, frac, 0.0))
        )
    select = jnp.concatenate(parts, 0).astype(jnp.bfloat16)
    lane = lax.broadcasted_iota(jnp.int32, (rows, LANES), 1)
    moves = []
    for place, direction in enumerate(wanted):
        steps = offsets_ref[direction, own, 1]
        start = steps >> 2
        frac = (steps & 3).astype(jnp.float32) * 0.25
        within = start & (LANES - 1)
        moves.append((start >> 7, within, (LANES - within) & (LANES - 1), frac))

    def columns(at):
        window = jnp.concatenate([block[:, at : at + GROUP] for block in blocks], 0)
        down = jnp.dot(select, window, preferred_element_type=jnp.float32)
        return [down[:, k : k + LANES] for k in range(0, GROUP, LANES)]

    wide = lax.broadcasted_iota(jnp.int32, (DIRS * rows, LANES), 1)

    def finish(place, k, here, after):
        skip, within = moves[place][:2]
        term = jnp.where(lane < LANES - within, here, after).astype(jnp.bfloat16)
        to = pl.ds(pl.multiple_of(((k - skip) & (PCOLS // LANES - 1)) * LANES, LANES), LANES)
        outs[place][:, to] = term

    def turned(value, ahead):
        out = []
        for place in range(DIRS):
            at = slice(place * rows, (place + 1) * rows)
            _, _, turn, frac = moves[place]
            out.append(pltpu.roll((1.0 - frac) * value[at] + frac * ahead[at], turn, 1))
        return out

    def shift(value):
        return pltpu.roll(value, LANES - 1, 1)

    count = PCOLS // LANES
    values, shifts, turns = {}, {}, {}

    def get(k):
        if k not in values:
            k -= k % (GROUP // LANES)
            for n, value in enumerate(columns(k * LANES)):
                values[k + n] = value
                shifts[k + n] = shift(value)

    get(0)
    for k in range(count):
        get((k + 1) % count)
        ahead = jnp.where(wide < LANES - 1, shifts[k], shifts[(k + 1) % count])
        turns[k] = turned(values[k], ahead)
        if k:
            for place in range(DIRS):
                finish(place, k - 1, turns[k - 1][place], turns[k][place])
    for place in range(DIRS):
        finish(place, count - 1, turns[count - 1][place], turns[0][place])


def terms(first, rows, index, offsets, blocks, carried=()):
    depths = tuple(b.shape[0] for b in blocks)
    flat = jax.ShapeDtypeStruct((rows, PCOLS), jnp.bfloat16)
    deep = jax.ShapeDtypeStruct((3, rows, PCOLS), jnp.bfloat16)
    outs = (flat, flat, deep) if carried else (flat,) * DIRS
    whole = pl.BlockSpec(memory_space=pltpu.VMEM)
    return pl.pallas_call(
        functools.partial(term_kernel, first, rows, depths, len(carried)),
        out_shape=outs,
        in_specs=[pl.BlockSpec(memory_space=pltpu.SMEM)] * 2
        + [whole] * (len(blocks) + len(carried)),
        out_specs=(whole,) * len(outs),
        compiler_params=pltpu.CompilerParams(vmem_limit_bytes=VMEM_LIMIT),
        cost_estimate=pl.CostEstimate(flops=1024, bytes_accessed=1024, transcendentals=0),
        name="terms",
    )(index, offsets, *blocks, *carried)


def series():
    points = 0.25 * (1.0 - np.cos(np.pi * (np.arange(4000) + 0.5) / 4000)) * 0.5
    basis = lambda count: np.stack([points**k for k in range(count)], 1)
    root = np.sqrt(points)
    sine = np.linalg.lstsq(basis(8), np.sin(2 * np.pi * root) / root, rcond=None)[0]
    cosine = np.linalg.lstsq(basis(8), np.cos(2 * np.pi * root), rcond=None)[0]
    return [float(c) for c in sine], [float(c) for c in cosine]


SINE, COSINE = series()


def horner(coefficients, square):
    value = jnp.full_like(square, coefficients[-1])
    for c in coefficients[-2::-1]:
        value = value * square + c
    return value


def final_kernel(chunks, grown, left_ref, right_ref, column_ref, *refs):
    keeps, pairs, fars = refs[:chunks], refs[chunks : 2 * chunks], refs[2 * chunks : 3 * chunks]
    out_ref = refs[3 * chunks + grown]
    cols = out_ref.shape[1]
    phase = jnp.concatenate(
        [
            (k[...].astype(jnp.float32) + p[0].astype(jnp.float32)) + f[...].astype(jnp.float32)
            for k, p, f in zip(keeps, pairs, fars)
        ],
        0,
    )
    turns = phase * (0.5 / math.pi)
    turns = turns - jnp.round(turns)
    square = turns * turns
    field = jnp.concatenate(
        [horner(COSINE, square), turns * horner(SINE, square)], 0
    ).astype(jnp.bfloat16)
    focal = jnp.dot(left_ref[...], field, preferred_element_type=jnp.float32)
    reals, imags = [], []
    for altitude in range(SLICES):
        real = focal[2 * SPOT * altitude : 2 * SPOT * altitude + SPOT]
        imag = focal[2 * SPOT * altitude + SPOT : 2 * SPOT * (altitude + 1)]
        cosine = column_ref[altitude : altitude + 1]
        sine = column_ref[SLICES + altitude : SLICES + altitude + 1]
        reals.append((real * cosine - imag * sine).astype(jnp.bfloat16))
        imags.append((real * sine + imag * cosine).astype(jnp.bfloat16))
    real = jnp.concatenate(reals, 0)
    imag = jnp.concatenate(imags, 0)
    for place in range(cols // SUBPIX):
        at = slice(place * SUBPIX, (place + 1) * SUBPIX)
        spot = jnp.dot(
            jnp.concatenate([real[:, at], imag[:, at]], 1),
            right_ref[...],
            preferred_element_type=jnp.float32,
        )
        power = spot * spot
        power = power[:, :SPOT] + power[:, SPOT:]
        total = None
        for altitude in range(SLICES):
            piece = power[altitude * SPOT : (altitude + 1) * SPOT]
            total = piece if total is None else total + piece
        lit = column_ref[2 * SLICES : 2 * SLICES + 1, at]
        out_ref[:, at] = (total * lit).astype(jnp.bfloat16)


def spots_of(left, right, column, keeps, pair, fars, start, width, whole):
    chunks = len(keeps)
    step = min(FINAL_COLS, width)
    at = start // step

    def part(array):
        skip = at if array.shape[1] == PCOLS else 0
        return pl.BlockSpec((array.shape[0], step), lambda i: (0, i + skip))

    deep = [
        pl.BlockSpec((1, pair.shape[1], step), lambda i, place=place: (place, 0, i + at))
        for place in (2, 1)
    ]
    taken = [column, *keeps, pair, pair, *fars]
    specs = [part(column), *map(part, keeps), *deep, *map(part, fars)]
    grown = [] if whole is None else [whole]
    return pl.pallas_call(
        functools.partial(final_kernel, chunks, len(grown)),
        grid=(width // step,),
        out_shape=jax.ShapeDtypeStruct((SPOT, PCOLS), jnp.bfloat16),
        in_specs=[
            pl.BlockSpec(left.shape, lambda i: (0, 0)),
            pl.BlockSpec(right.shape, lambda i: (0, 0)),
            *specs,
            *(pl.BlockSpec(memory_space=pl.ANY) for _ in grown),
        ],
        out_specs=pl.BlockSpec((SPOT, step), lambda i: (0, i + at)),
        input_output_aliases={2 + len(taken): 0} if grown else {},
        compiler_params=pltpu.CompilerParams(vmem_limit_bytes=VMEM_LIMIT),
        cost_estimate=pl.CostEstimate(flops=1024, bytes_accessed=1024, transcendentals=0),
        name="spots",
    )(left, right, *taken, *grown)


def shards(layers, offsets, subap_valid, defocus, weights):
    index = lax.axis_index("dir").astype(jnp.int32)[None]
    tile = lax.axis_index("tile")
    total_rows = lax.axis_size("tile") * SUBPIX
    block = layers[0]
    own = [block[: CUTS[1]], lax.optimization_barrier(block)[CUTS[1] :]]
    once = [shifted(piece, -1) for piece in own]

    real_part, imag_part, right = tables()
    row = (
        (tile * SUBPIX + jnp.arange(SUBPIX, dtype=jnp.int32)).astype(jnp.float32)
        - (total_rows - 1) / 2.0
    ) / SUBPIX
    col = (jnp.arange(PCOLS, dtype=jnp.float32) - (PCOLS - 1) / 2.0) / SUBPIX
    row_angle = defocus[:, None] * (row * row)[None, :]
    col_angle = defocus[:, None] * (col * col)[None, :]
    row_cos, row_sin = jnp.cos(row_angle)[:, None], jnp.sin(row_angle)[:, None]
    left_real = real_part[None] * row_cos - imag_part[None] * row_sin
    left_imag = real_part[None] * row_sin + imag_part[None] * row_cos
    left = jnp.concatenate(
        [
            jnp.concatenate([left_real, -left_imag], 2),
            jnp.concatenate([left_imag, left_real], 2),
        ],
        1,
    )
    left = left.reshape(SLICES * 2 * SPOT, 2 * SUBPIX).astype(jnp.bfloat16)
    share = jnp.sqrt(weights / jnp.sum(weights))[:, None]
    lit = jnp.repeat(subap_valid.astype(jnp.float32), SUBPIX, axis=1)
    column = jnp.concatenate([jnp.cos(col_angle) * share, jnp.sin(col_angle) * share, lit], 0)

    once[0], offsets, left, column = lax.optimization_barrier((once[0], offsets, left, column))
    twice = [shifted(piece, -1) for piece in once]

    blocks = own + once + twice[:1]
    keep, send, cross, cross_send = terms(0, CUTS[1], index, offsets, blocks)
    joined = other_core(cross_send)
    joined, twice[1] = lax.optimization_barrier((joined, twice[1]))
    both = (send.astype(jnp.float32) + joined.astype(jnp.float32)).astype(jnp.bfloat16)
    keeps, fars = [keep], [other_chip(both)]

    blocks = own[1:] + once + twice
    keep, send, crosses = terms(CUTS[1], CUTS[2] - CUTS[1], index, offsets, blocks, (cross,))
    keeps.append(keep)
    pair = other_core(crosses)
    sides = []
    for a, b in zip(SIDES, SIDES[1:]):
        both = send[:, a:b].astype(jnp.float32) + pair[0, :, a:b].astype(jnp.float32)
        sides.append(other_chip(both.astype(jnp.bfloat16)))

    spots = None
    for side, a, b in zip(sides, SIDES, SIDES[1:]):
        spots = spots_of(left, right, column, keeps, pair, fars + [side], a, b - a, spots)
    return spots[None, None]


def solution(mesh):
    placed = (P("dir", "tile", None), P(), P("tile", None), P(), P())
    return jax.shard_map(
        shards, mesh=mesh, in_specs=placed, out_specs=P("dir", "tile", None, None), check_vma=False
    )
```

```python
import functools
import math

import jax
import jax.numpy as jnp
import numpy as np
from jax import lax
from jax.experimental import pallas as pl
from jax.experimental.pallas import tpu as pltpu
from jax.sharding import PartitionSpec as P

SUBPIX = 128
SPOT = 128
SUBX = 16
SLICES = 3
QUANT = 4
OVER = 2
PCOLS = 2048
DIRS = 4

CUTS = (0, 64, 128)
SIDES = (0, 1024, 2048)
FINAL_COLS = 1024
LANES = 128
BAND = 256
GROUP = 256
VMEM_LIMIT = 48 * 1024 * 1024


def tables():
    frequency = np.arange(SPOT, dtype=np.float64) - SPOT // 2
    position = np.arange(SUBPIX, dtype=np.float64) - (SUBPIX - 1) / 2.0
    angle = -2.0 * math.pi / (OVER * SUBPIX) * frequency[:, None] * position[None, :]
    factor = 1.0 / math.sqrt(SUBPIX)
    real_part = (np.cos(angle) * factor).astype(jnp.bfloat16)
    imag_part = (np.sin(angle) * factor).astype(jnp.bfloat16)
    right = np.block([[real_part.T, imag_part.T], [-imag_part.T, real_part.T]])
    return real_part.astype(np.float32), imag_part.astype(np.float32), right


def shifted(value, by):
    count = lax.axis_size("tile")
    return lax.ppermute(value, "tile", [(i, (i + by) % count) for i in range(count)])


def other_core(value):
    return lax.ppermute(value, "dir", [(0, 1), (1, 0), (2, 3), (3, 2)])


def other_chip(value):
    return lax.ppermute(value, "dir", [(0, 2), (1, 3), (2, 0), (3, 1)])


def term_kernel(first, rows, depths, carried, index_ref, offsets_ref, *refs):
    blocks = refs[: len(depths)]
    outs = refs[len(depths) + carried :]
    if carried:
        outs[2][2 * rows :] = refs[len(depths)][...]
        outs = (*outs[:2], outs[2].at[rows : 2 * rows], outs[2].at[:rows])
    total = sum(depths)
    own = index_ref[0]
    wanted = (own, own ^ 2, own ^ 1, own ^ 3)
    parts = []
    for direction in wanted:
        steps = offsets_ref[direction, own, 0]
        start = steps >> 2
        frac = (steps & 3).astype(jnp.float32) * 0.25
        away = lax.broadcasted_iota(jnp.int32, (rows, total), 1) - lax.broadcasted_iota(
            jnp.int32, (rows, total), 0
        )
        parts.append(
            jnp.where(away == start, 1.0 - frac, jnp.where(away == start + 1, frac, 0.0))
        )
    select = jnp.concatenate(parts, 0).astype(jnp.bfloat16)
    lane = lax.broadcasted_iota(jnp.int32, (rows, LANES), 1)
    moves = []
    for place, direction in enumerate(wanted):
        steps = offsets_ref[direction, own, 1]
        start = steps >> 2
        frac = (steps & 3).astype(jnp.float32) * 0.25
        within = start & (LANES - 1)
        moves.append((start >> 7, within, (LANES - within) & (LANES - 1), frac))

    def columns(at):
        window = jnp.concatenate([block[:, at : at + GROUP] for block in blocks], 0)
        down = jnp.dot(select, window, preferred_element_type=jnp.float32)
        return [down[:, k : k + LANES] for k in range(0, GROUP, LANES)]

    wide = lax.broadcasted_iota(jnp.int32, (DIRS * rows, LANES), 1)

    def finish(place, k, here, after):
        skip, within = moves[place][:2]
        term = jnp.where(lane < LANES - within, here, after).astype(jnp.bfloat16)
        to = pl.ds(pl.multiple_of(((k - skip) & (PCOLS // LANES - 1)) * LANES, LANES), LANES)
        outs[place][:, to] = term

    def turned(value, ahead):
        out = []
        for place in range(DIRS):
            at = slice(place * rows, (place + 1) * rows)
            _, _, turn, frac = moves[place]
            out.append(pltpu.roll((1.0 - frac) * value[at] + frac * ahead[at], turn, 1))
        return out

    def shift(value):
        return pltpu.roll(value, LANES - 1, 1)

    count = PCOLS // LANES
    values, shifts, turns = {}, {}, {}

    def get(k):
        if k not in values:
            k -= k % (GROUP // LANES)
            for n, value in enumerate(columns(k * LANES)):
                values[k + n] = value
                shifts[k + n] = shift(value)

    get(0)
    for k in range(count):
        get((k + 1) % count)
        ahead = jnp.where(wide < LANES - 1, shifts[k], shifts[(k + 1) % count])
        turns[k] = turned(values[k], ahead)
        if k:
            for place in range(DIRS):
                finish(place, k - 1, turns[k - 1][place], turns[k][place])
    for place in range(DIRS):
        finish(place, count - 1, turns[count - 1][place], turns[0][place])


def terms(first, rows, index, offsets, blocks, carried=()):
    depths = tuple(b.shape[0] for b in blocks)
    flat = jax.ShapeDtypeStruct((rows, PCOLS), jnp.bfloat16)
    outs = (flat,) * DIRS
    if carried:
        deep = 2 * rows + carried[0].shape[0]
        outs = (flat, flat, jax.ShapeDtypeStruct((deep, PCOLS), jnp.bfloat16))
    whole = pl.BlockSpec(memory_space=pltpu.VMEM)
    return pl.pallas_call(
        functools.partial(term_kernel, first, rows, depths, len(carried)),
        out_shape=outs,
        in_specs=[pl.BlockSpec(memory_space=pltpu.SMEM)] * 2
        + [whole] * (len(blocks) + len(carried)),
        out_specs=(whole,) * len(outs),
        compiler_params=pltpu.CompilerParams(vmem_limit_bytes=VMEM_LIMIT),
        cost_estimate=pl.CostEstimate(flops=1024, bytes_accessed=1024, transcendentals=0),
        name="terms",
    )(index, offsets, *blocks, *carried)


def series():
    points = 0.25 * (1.0 - np.cos(np.pi * (np.arange(4000) + 0.5) / 4000)) * 0.5
    basis = lambda count: np.stack([points**k for k in range(count)], 1)
    root = np.sqrt(points)
    sine = np.linalg.lstsq(basis(8), np.sin(2 * np.pi * root) / root, rcond=None)[0]
    cosine = np.linalg.lstsq(basis(8), np.cos(2 * np.pi * root), rcond=None)[0]
    return [float(c) for c in sine], [float(c) for c in cosine]


SINE, COSINE = series()


def horner(coefficients, square):
    value = jnp.full_like(square, coefficients[-1])
    for c in coefficients[-2::-1]:
        value = value * square + c
    return value


def final_kernel(chunks, grown, left_ref, right_ref, column_ref, *refs):
    keeps, pair_ref, fars = refs[:chunks], refs[chunks], refs[chunks + 1 : 2 * chunks + 1]
    out_ref = refs[2 * chunks + 1 + grown]
    last = keeps[1].shape[0]
    pairs = (slice(2 * last, None), slice(last, 2 * last))
    for at in range(0, out_ref.shape[1], BAND):
        band = slice(at, at + BAND)
        phase = jnp.concatenate(
            [
                (k[:, band].astype(jnp.float32) + pair_ref[p, band].astype(jnp.float32))
                + f[:, band].astype(jnp.float32)
                for k, p, f in zip(keeps, pairs, fars)
            ],
            0,
        )
        turns = phase * (0.5 / math.pi)
        turns = turns - jnp.round(turns)
        square = turns * turns
        field = jnp.concatenate(
            [horner(COSINE, square), turns * horner(SINE, square)], 0
        ).astype(jnp.bfloat16)
        focal = jnp.dot(left_ref[...], field, preferred_element_type=jnp.float32)
        reals, imags = [], []
        for altitude in range(SLICES):
            real = focal[2 * SPOT * altitude : 2 * SPOT * altitude + SPOT]
            imag = focal[2 * SPOT * altitude + SPOT : 2 * SPOT * (altitude + 1)]
            cosine = column_ref[altitude : altitude + 1, band]
            sine = column_ref[SLICES + altitude : SLICES + altitude + 1, band]
            reals.append((real * cosine - imag * sine).astype(jnp.bfloat16))
            imags.append((real * sine + imag * cosine).astype(jnp.bfloat16))
        real = jnp.concatenate(reals, 0)
        imag = jnp.concatenate(imags, 0)
        for place in range(0, BAND, SUBPIX):
            spot = jnp.dot(
                jnp.concatenate([real[:, place : place + SUBPIX], imag[:, place : place + SUBPIX]], 1),
                right_ref[...],
                preferred_element_type=jnp.float32,
            )
            power = spot * spot
            power = power[:, :SPOT] + power[:, SPOT:]
            total = power[:SPOT]
            for altitude in range(1, SLICES):
                total = total + power[altitude * SPOT : (altitude + 1) * SPOT]
            to = slice(at + place, at + place + SUBPIX)
            lit = column_ref[2 * SLICES : 2 * SLICES + 1, to]
            out_ref[:, to] = (total * lit).astype(jnp.bfloat16)


def spots_of(left, right, column, keeps, pair, fars, start, width, whole):
    chunks = len(keeps)
    step = min(FINAL_COLS, width)
    at = start // step

    def part(array):
        skip = at if array.shape[1] == PCOLS else 0
        return pl.BlockSpec((array.shape[0], step), lambda i: (0, i + skip))

    taken = [column, *keeps, pair, *fars]
    grown = [] if whole is None else [whole]
    return pl.pallas_call(
        functools.partial(final_kernel, chunks, len(grown)),
        grid=(width // step,),
        out_shape=jax.ShapeDtypeStruct((SPOT, PCOLS), jnp.bfloat16),
        in_specs=[
            pl.BlockSpec(left.shape, lambda i: (0, 0)),
            pl.BlockSpec(right.shape, lambda i: (0, 0)),
            *map(part, taken),
            *(pl.BlockSpec(memory_space=pl.ANY) for _ in grown),
        ],
        out_specs=pl.BlockSpec((SPOT, step), lambda i: (0, i + at)),
        input_output_aliases={2 + len(taken): 0} if grown else {},
        compiler_params=pltpu.CompilerParams(vmem_limit_bytes=VMEM_LIMIT),
        cost_estimate=pl.CostEstimate(flops=1024, bytes_accessed=1024, transcendentals=0),
        name="spots",
    )(left, right, *taken, *grown)


def shards(layers, offsets, subap_valid, defocus, weights):
    index = lax.axis_index("dir").astype(jnp.int32)[None]
    tile = lax.axis_index("tile")
    total_rows = lax.axis_size("tile") * SUBPIX
    block = layers[0]
    own = [block[: CUTS[1]]]
    once = [shifted(own[0], -1)]

    real_part, imag_part, right = tables()
    row = (
        (tile * SUBPIX + jnp.arange(SUBPIX, dtype=jnp.int32)).astype(jnp.float32)
        - (total_rows - 1) / 2.0
    ) / SUBPIX
    col = (jnp.arange(PCOLS, dtype=jnp.float32) - (PCOLS - 1) / 2.0) / SUBPIX
    row_angle = defocus[:, None] * (row * row)[None, :]
    col_angle = defocus[:, None] * (col * col)[None, :]
    row_cos, row_sin = jnp.cos(row_angle)[:, None], jnp.sin(row_angle)[:, None]
    left_real = real_part[None] * row_cos - imag_part[None] * row_sin
    left_imag = real_part[None] * row_sin + imag_part[None] * row_cos
    left = jnp.concatenate(
        [
            jnp.concatenate([left_real, -left_imag], 2),
            jnp.concatenate([left_imag, left_real], 2),
        ],
        1,
    )
    left = left.reshape(SLICES * 2 * SPOT, 2 * SUBPIX).astype(jnp.bfloat16)
    share = jnp.sqrt(weights / jnp.sum(weights))[:, None]
    lit = jnp.repeat(subap_valid.astype(jnp.float32), SUBPIX, axis=1)
    column = jnp.concatenate([jnp.cos(col_angle) * share, jnp.sin(col_angle) * share, lit], 0)

    block, left = lax.optimization_barrier((block, left))
    own.append(block[CUTS[1] :])
    once.append(shifted(own[1], -1))
    once[0], offsets, column = lax.optimization_barrier((once[0], offsets, column))
    twice = [shifted(piece, -1) for piece in once]

    blocks = own + once + twice[:1]
    keep, send, cross, cross_send = terms(0, CUTS[1], index, offsets, blocks)
    joined = other_core(cross_send)
    joined, twice[1] = lax.optimization_barrier((joined, twice[1]))
    both = (send.astype(jnp.float32) + joined.astype(jnp.float32)).astype(jnp.bfloat16)
    keeps, fars = [keep], [other_chip(both)]

    blocks = own[1:] + once + twice
    keep, send, crosses = terms(CUTS[1], CUTS[2] - CUTS[1], index, offsets, blocks, (cross,))
    keeps.append(keep)
    pair = other_core(crosses)
    sides = []
    for a, b in zip(SIDES, SIDES[1:]):
        both = send[:, a:b].astype(jnp.float32) + pair[: send.shape[0], a:b].astype(jnp.float32)
        sides.append(other_chip(both.astype(jnp.bfloat16)))

    spots = None
    for side, a, b in zip(sides, SIDES, SIDES[1:]):
        spots = spots_of(left, right, column, keeps, pair, fars + [side], a, b - a, spots)
    return spots[None, None]


def solution(mesh):
    placed = (P("dir", "tile", None), P(), P("tile", None), P(), P())
    return jax.shard_map(
        shards, mesh=mesh, in_specs=placed, out_specs=P("dir", "tile", None, None), check_vma=False
    )
```

```python
import functools
import math

import jax
import jax.numpy as jnp
import numpy as np
from jax import lax
from jax.experimental import pallas as pl
from jax.experimental.pallas import tpu as pltpu
from jax.sharding import PartitionSpec as P

SUBPIX = 128
SPOT = 128
SUBX = 16
SLICES = 3
QUANT = 4
OVER = 2
PCOLS = 2048
DIRS = 4

CUTS = (0, 64, 128)
SIDES = (0, 1024, 2048)
FINAL_COLS = 1024
LANES = 128
BAND = 256
GROUP = 256
VMEM_LIMIT = 48 * 1024 * 1024


def tables():
    frequency = np.arange(SPOT, dtype=np.float64) - SPOT // 2
    position = np.arange(SUBPIX, dtype=np.float64) - (SUBPIX - 1) / 2.0
    angle = -2.0 * math.pi / (OVER * SUBPIX) * frequency[:, None] * position[None, :]
    factor = 1.0 / math.sqrt(SUBPIX)
    real_part = (np.cos(angle) * factor).astype(jnp.bfloat16)
    imag_part = (np.sin(angle) * factor).astype(jnp.bfloat16)
    right = np.block([[real_part.T, imag_part.T], [-imag_part.T, real_part.T]])
    return real_part.astype(np.float32), imag_part.astype(np.float32), right


def shifted(value, by):
    count = lax.axis_size("tile")
    return lax.ppermute(value, "tile", [(i, (i + by) % count) for i in range(count)])


def other_core(value):
    return lax.ppermute(value, "dir", [(0, 1), (1, 0), (2, 3), (3, 2)])


def other_chip(value):
    return lax.ppermute(value, "dir", [(0, 2), (1, 3), (2, 0), (3, 1)])


def term_kernel(first, rows, depths, carried, index_ref, offsets_ref, *refs):
    blocks = refs[: len(depths)]
    outs = refs[len(depths) + carried :]
    if carried:
        outs[2][2 * rows :] = refs[len(depths)][...]
        outs = (*outs[:2], outs[2].at[rows : 2 * rows], outs[2].at[:rows])
    total = sum(depths)
    own = index_ref[0]
    wanted = (own, own ^ 2, own ^ 1, own ^ 3)
    parts = []
    for direction in wanted:
        steps = offsets_ref[direction, own, 0]
        start = steps >> 2
        frac = (steps & 3).astype(jnp.float32) * 0.25
        away = lax.broadcasted_iota(jnp.int32, (rows, total), 1) - lax.broadcasted_iota(
            jnp.int32, (rows, total), 0
        )
        parts.append(
            jnp.where(away == start, 1.0 - frac, jnp.where(away == start + 1, frac, 0.0))
        )
    select = jnp.concatenate(parts, 0).astype(jnp.bfloat16)
    lane = lax.broadcasted_iota(jnp.int32, (rows, LANES), 1)
    moves = []
    for place, direction in enumerate(wanted):
        steps = offsets_ref[direction, own, 1]
        start = steps >> 2
        frac = (steps & 3).astype(jnp.float32) * 0.25
        within = start & (LANES - 1)
        moves.append((start >> 7, within, (LANES - within) & (LANES - 1), frac))

    def columns(at):
        window = jnp.concatenate([block[:, at : at + GROUP] for block in blocks], 0)
        down = jnp.dot(select, window, preferred_element_type=jnp.float32)
        return [down[:, k : k + LANES] for k in range(0, GROUP, LANES)]

    wide = lax.broadcasted_iota(jnp.int32, (DIRS * rows, LANES), 1)

    def finish(place, k, here, after):
        skip, within = moves[place][:2]
        term = jnp.where(lane < LANES - within, here, after).astype(jnp.bfloat16)
        to = pl.ds(pl.multiple_of(((k - skip) & (PCOLS // LANES - 1)) * LANES, LANES), LANES)
        outs[place][:, to] = term

    def turned(value, ahead):
        out = []
        for place in range(DIRS):
            at = slice(place * rows, (place + 1) * rows)
            _, _, turn, frac = moves[place]
            out.append(pltpu.roll((1.0 - frac) * value[at] + frac * ahead[at], turn, 1))
        return out

    def shift(value):
        return pltpu.roll(value, LANES - 1, 1)

    count = PCOLS // LANES
    values, shifts, turns = {}, {}, {}

    def get(k):
        if k not in values:
            k -= k % (GROUP // LANES)
            for n, value in enumerate(columns(k * LANES)):
                values[k + n] = value
                shifts[k + n] = shift(value)

    get(0)
    for k in range(count):
        get((k + 1) % count)
        ahead = jnp.where(wide < LANES - 1, shifts[k], shifts[(k + 1) % count])
        turns[k] = turned(values[k], ahead)
        if k:
            for place in range(DIRS):
                finish(place, k - 1, turns[k - 1][place], turns[k][place])
    for place in range(DIRS):
        finish(place, count - 1, turns[count - 1][place], turns[0][place])


def terms(first, rows, index, offsets, blocks, carried=()):
    depths = tuple(b.shape[0] for b in blocks)
    flat = jax.ShapeDtypeStruct((rows, PCOLS), jnp.bfloat16)
    outs = (flat,) * DIRS
    if carried:
        deep = 2 * rows + carried[0].shape[0]
        outs = (flat, flat, jax.ShapeDtypeStruct((deep, PCOLS), jnp.bfloat16))
    whole = pl.BlockSpec(memory_space=pltpu.VMEM)
    return pl.pallas_call(
        functools.partial(term_kernel, first, rows, depths, len(carried)),
        out_shape=outs,
        in_specs=[pl.BlockSpec(memory_space=pltpu.SMEM)] * 2
        + [whole] * (len(blocks) + len(carried)),
        out_specs=(whole,) * len(outs),
        compiler_params=pltpu.CompilerParams(vmem_limit_bytes=VMEM_LIMIT),
        cost_estimate=pl.CostEstimate(flops=1024, bytes_accessed=1024, transcendentals=0),
        name="terms",
    )(index, offsets, *blocks, *carried)


def series():
    points = 0.25 * (1.0 - np.cos(np.pi * (np.arange(4000) + 0.5) / 4000)) * 0.5
    basis = lambda count: np.stack([points**k for k in range(count)], 1)
    root = np.sqrt(points)
    sine = np.linalg.lstsq(basis(8), np.sin(2 * np.pi * root) / root, rcond=None)[0]
    cosine = np.linalg.lstsq(basis(8), np.cos(2 * np.pi * root), rcond=None)[0]
    return [float(c) for c in sine], [float(c) for c in cosine]


SINE, COSINE = series()


def horner(coefficients, square):
    value = jnp.full_like(square, coefficients[-1])
    for c in coefficients[-2::-1]:
        value = value * square + c
    return value


def final_kernel(chunks, grown, left_ref, right_ref, column_ref, *refs):
    keeps, pair_ref, fars = refs[:chunks], refs[chunks], refs[chunks + 1 : 2 * chunks + 1]
    out_ref = refs[2 * chunks + 1 + grown]
    last = keeps[1].shape[0]
    pairs = (slice(2 * last, None), slice(last, 2 * last))
    for at in range(0, out_ref.shape[1], BAND):
        band = slice(at, at + BAND)
        phase = jnp.concatenate(
            [
                (k[:, band].astype(jnp.float32) + pair_ref[p, band].astype(jnp.float32))
                + f[:, band].astype(jnp.float32)
                for k, p, f in zip(keeps, pairs, fars)
            ],
            0,
        )
        turns = phase * (0.5 / math.pi)
        turns = turns - jnp.round(turns)
        square = turns * turns
        field = jnp.concatenate(
            [horner(COSINE, square), turns * horner(SINE, square)], 0
        ).astype(jnp.bfloat16)
        focal = jnp.dot(left_ref[...], field, preferred_element_type=jnp.float32)
        reals, imags = [], []
        for altitude in range(SLICES):
            real = focal[2 * SPOT * altitude : 2 * SPOT * altitude + SPOT]
            imag = focal[2 * SPOT * altitude + SPOT : 2 * SPOT * (altitude + 1)]
            cosine = column_ref[altitude : altitude + 1, band]
            sine = column_ref[SLICES + altitude : SLICES + altitude + 1, band]
            reals.append((real * cosine - imag * sine).astype(jnp.bfloat16))
            imags.append((real * sine + imag * cosine).astype(jnp.bfloat16))
        real = jnp.concatenate(reals, 0)
        imag = jnp.concatenate(imags, 0)
        for place in range(0, BAND, SUBPIX):
            spot = jnp.dot(
                jnp.concatenate([real[:, place : place + SUBPIX], imag[:, place : place + SUBPIX]], 1),
                right_ref[...],
                preferred_element_type=jnp.float32,
            )
            power = spot * spot
            power = power[:, :SPOT] + power[:, SPOT:]
            total = power[:SPOT]
            for altitude in range(1, SLICES):
                total = total + power[altitude * SPOT : (altitude + 1) * SPOT]
            to = slice(at + place, at + place + SUBPIX)
            lit = column_ref[2 * SLICES : 2 * SLICES + 1, to]
            out_ref[:, to] = (total * lit).astype(jnp.bfloat16)


def spots_of(left, right, column, keeps, pair, fars, start, width, whole):
    chunks = len(keeps)
    step = min(FINAL_COLS, width)
    at = start // step

    def part(array):
        skip = at if array.shape[1] == PCOLS else 0
        return pl.BlockSpec((array.shape[0], step), lambda i: (0, i + skip))

    taken = [column, *keeps, pair, *fars]
    grown = [] if whole is None else [whole]
    return pl.pallas_call(
        functools.partial(final_kernel, chunks, len(grown)),
        grid=(width // step,),
        out_shape=jax.ShapeDtypeStruct((SPOT, PCOLS), jnp.bfloat16),
        in_specs=[
            pl.BlockSpec(left.shape, lambda i: (0, 0)),
            pl.BlockSpec(right.shape, lambda i: (0, 0)),
            *map(part, taken),
            *(pl.BlockSpec(memory_space=pl.ANY) for _ in grown),
        ],
        out_specs=pl.BlockSpec((SPOT, step), lambda i: (0, i + at)),
        input_output_aliases={2 + len(taken): 0} if grown else {},
        compiler_params=pltpu.CompilerParams(vmem_limit_bytes=VMEM_LIMIT),
        cost_estimate=pl.CostEstimate(flops=1024, bytes_accessed=1024, transcendentals=0),
        name="spots",
    )(left, right, *taken, *grown)


def shards(layers, offsets, subap_valid, defocus, weights):
    index = lax.axis_index("dir").astype(jnp.int32)[None]
    tile = lax.axis_index("tile")
    total_rows = lax.axis_size("tile") * SUBPIX
    block = layers[0]
    own = [block[: CUTS[1]]]
    once = [shifted(own[0], -1)]

    real_part, imag_part, right = tables()
    row = (
        (tile * SUBPIX + jnp.arange(SUBPIX, dtype=jnp.int32)).astype(jnp.float32)
        - (total_rows - 1) / 2.0
    ) / SUBPIX
    col = (jnp.arange(PCOLS, dtype=jnp.float32) - (PCOLS - 1) / 2.0) / SUBPIX
    row_angle = defocus[:, None] * (row * row)[None, :]
    col_angle = defocus[:, None] * (col * col)[None, :]
    row_cos, row_sin = jnp.cos(row_angle)[:, None], jnp.sin(row_angle)[:, None]
    left_real = real_part[None] * row_cos - imag_part[None] * row_sin
    left_imag = real_part[None] * row_sin + imag_part[None] * row_cos
    left = jnp.concatenate(
        [
            jnp.concatenate([left_real, -left_imag], 2),
            jnp.concatenate([left_imag, left_real], 2),
        ],
        1,
    )
    left = left.reshape(SLICES * 2 * SPOT, 2 * SUBPIX).astype(jnp.bfloat16)
    share = jnp.sqrt(weights / jnp.sum(weights))[:, None]
    lit = jnp.repeat(subap_valid.astype(jnp.float32), SUBPIX, axis=1)
    column = jnp.concatenate([jnp.cos(col_angle) * share, jnp.sin(col_angle) * share, lit], 0)

    block = lax.optimization_barrier(block)
    own.append(block[CUTS[1] :])
    once.append(shifted(own[1], -1))
    once[0], offsets, column, left = lax.optimization_barrier((once[0], offsets, column, left))
    twice = [shifted(piece, -1) for piece in once]

    blocks = own + once + twice[:1]
    keep, send, cross, cross_send = terms(0, CUTS[1], index, offsets, blocks)
    joined = other_core(cross_send)
    joined, twice[1] = lax.optimization_barrier((joined, twice[1]))
    both = (send.astype(jnp.float32) + joined.astype(jnp.float32)).astype(jnp.bfloat16)
    keeps, fars = [keep], [other_chip(both)]

    blocks = own[1:] + once + twice
    keep, send, crosses = terms(CUTS[1], CUTS[2] - CUTS[1], index, offsets, blocks, (cross,))
    keeps.append(keep)
    pair = other_core(crosses)
    sides = []
    for a, b in zip(SIDES, SIDES[1:]):
        both = send[:, a:b].astype(jnp.float32) + pair[: send.shape[0], a:b].astype(jnp.float32)
        sides.append(other_chip(both.astype(jnp.bfloat16)))

    spots = None
    for side, a, b in zip(sides, SIDES, SIDES[1:]):
        spots = spots_of(left, right, column, keeps, pair, fars + [side], a, b - a, spots)
    return spots[None, None]


def solution(mesh):
    placed = (P("dir", "tile", None), P(), P("tile", None), P(), P())
    return jax.shard_map(
        shards, mesh=mesh, in_specs=placed, out_specs=P("dir", "tile", None, None), check_vma=False
    )
```

```python
import functools
import math

import jax
import jax.numpy as jnp
import numpy as np
from jax import lax
from jax.experimental import pallas as pl
from jax.experimental.pallas import tpu as pltpu
from jax.sharding import PartitionSpec as P

SUBPIX = 128
SPOT = 128
SUBX = 16
SLICES = 3
QUANT = 4
OVER = 2
PCOLS = 2048
DIRS = 4

CUTS = (0, 48, 128)
SIDES = (0, 1024, 2048)
FINAL_COLS = 1024
LANES = 128
BAND = 256
GROUP = 256
VMEM_LIMIT = 48 * 1024 * 1024


def tables():
    frequency = np.arange(SPOT, dtype=np.float64) - SPOT // 2
    position = np.arange(SUBPIX, dtype=np.float64) - (SUBPIX - 1) / 2.0
    angle = -2.0 * math.pi / (OVER * SUBPIX) * frequency[:, None] * position[None, :]
    factor = 1.0 / math.sqrt(SUBPIX)
    real_part = (np.cos(angle) * factor).astype(jnp.bfloat16)
    imag_part = (np.sin(angle) * factor).astype(jnp.bfloat16)
    right = np.block([[real_part.T, imag_part.T], [-imag_part.T, real_part.T]])
    return real_part.astype(np.float32), imag_part.astype(np.float32), right


def shifted(value, by):
    count = lax.axis_size("tile")
    return lax.ppermute(value, "tile", [(i, (i + by) % count) for i in range(count)])


def other_core(value):
    return lax.ppermute(value, "dir", [(0, 1), (1, 0), (2, 3), (3, 2)])


def other_chip(value):
    return lax.ppermute(value, "dir", [(0, 2), (1, 3), (2, 0), (3, 1)])


def term_kernel(first, rows, depths, carried, index_ref, offsets_ref, *refs):
    blocks = refs[: len(depths)]
    outs = refs[len(depths) + carried :]
    if carried:
        outs[2][2 * rows :] = refs[len(depths)][...]
        outs = (*outs[:2], outs[2].at[rows : 2 * rows], outs[2].at[:rows])
    total = sum(depths)
    own = index_ref[0]
    wanted = (own, own ^ 2, own ^ 1, own ^ 3)
    parts = []
    for direction in wanted:
        steps = offsets_ref[direction, own, 0]
        start = steps >> 2
        frac = (steps & 3).astype(jnp.float32) * 0.25
        away = lax.broadcasted_iota(jnp.int32, (rows, total), 1) - lax.broadcasted_iota(
            jnp.int32, (rows, total), 0
        )
        parts.append(
            jnp.where(away == start, 1.0 - frac, jnp.where(away == start + 1, frac, 0.0))
        )
    select = jnp.concatenate(parts, 0).astype(jnp.bfloat16)
    lane = lax.broadcasted_iota(jnp.int32, (rows, LANES), 1)
    moves = []
    for place, direction in enumerate(wanted):
        steps = offsets_ref[direction, own, 1]
        start = steps >> 2
        frac = (steps & 3).astype(jnp.float32) * 0.25
        within = start & (LANES - 1)
        moves.append((start >> 7, within, (LANES - within) & (LANES - 1), frac))

    def columns(at):
        window = jnp.concatenate([block[:, at : at + GROUP] for block in blocks], 0)
        down = jnp.dot(select, window, preferred_element_type=jnp.float32)
        return [down[:, k : k + LANES] for k in range(0, GROUP, LANES)]

    wide = lax.broadcasted_iota(jnp.int32, (DIRS * rows, LANES), 1)

    def finish(place, k, here, after):
        skip, within = moves[place][:2]
        term = jnp.where(lane < LANES - within, here, after).astype(jnp.bfloat16)
        to = pl.ds(pl.multiple_of(((k - skip) & (PCOLS // LANES - 1)) * LANES, LANES), LANES)
        outs[place][:, to] = term

    def turned(value, ahead):
        out = []
        for place in range(DIRS):
            at = slice(place * rows, (place + 1) * rows)
            _, _, turn, frac = moves[place]
            out.append(pltpu.roll((1.0 - frac) * value[at] + frac * ahead[at], turn, 1))
        return out

    def shift(value):
        return pltpu.roll(value, LANES - 1, 1)

    count = PCOLS // LANES
    values, shifts, turns = {}, {}, {}

    def get(k):
        if k not in values:
            k -= k % (GROUP // LANES)
            for n, value in enumerate(columns(k * LANES)):
                values[k + n] = value
                shifts[k + n] = shift(value)

    get(0)
    for k in range(count):
        get((k + 1) % count)
        ahead = jnp.where(wide < LANES - 1, shifts[k], shifts[(k + 1) % count])
        turns[k] = turned(values[k], ahead)
        if k:
            for place in range(DIRS):
                finish(place, k - 1, turns[k - 1][place], turns[k][place])
    for place in range(DIRS):
        finish(place, count - 1, turns[count - 1][place], turns[0][place])


def terms(first, rows, index, offsets, blocks, carried=()):
    depths = tuple(b.shape[0] for b in blocks)
    flat = jax.ShapeDtypeStruct((rows, PCOLS), jnp.bfloat16)
    outs = (flat,) * DIRS
    if carried:
        deep = 2 * rows + carried[0].shape[0]
        outs = (flat, flat, jax.ShapeDtypeStruct((deep, PCOLS), jnp.bfloat16))
    whole = pl.BlockSpec(memory_space=pltpu.VMEM)
    return pl.pallas_call(
        functools.partial(term_kernel, first, rows, depths, len(carried)),
        out_shape=outs,
        in_specs=[pl.BlockSpec(memory_space=pltpu.SMEM)] * 2
        + [whole] * (len(blocks) + len(carried)),
        out_specs=(whole,) * len(outs),
        compiler_params=pltpu.CompilerParams(vmem_limit_bytes=VMEM_LIMIT),
        cost_estimate=pl.CostEstimate(flops=1024, bytes_accessed=1024, transcendentals=0),
        name="terms",
    )(index, offsets, *blocks, *carried)


def series():
    points = 0.25 * (1.0 - np.cos(np.pi * (np.arange(4000) + 0.5) / 4000)) * 0.5
    basis = lambda count: np.stack([points**k for k in range(count)], 1)
    root = np.sqrt(points)
    sine = np.linalg.lstsq(basis(8), np.sin(2 * np.pi * root) / root, rcond=None)[0]
    cosine = np.linalg.lstsq(basis(8), np.cos(2 * np.pi * root), rcond=None)[0]
    return [float(c) for c in sine], [float(c) for c in cosine]


SINE, COSINE = series()


def horner(coefficients, square):
    value = jnp.full_like(square, coefficients[-1])
    for c in coefficients[-2::-1]:
        value = value * square + c
    return value


def final_kernel(chunks, grown, left_ref, right_ref, column_ref, *refs):
    keeps, pair_ref, fars = refs[:chunks], refs[chunks], refs[chunks + 1 : 2 * chunks + 1]
    out_ref = refs[2 * chunks + 1 + grown]
    last = keeps[1].shape[0]
    pairs = (slice(2 * last, None), slice(last, 2 * last))
    for at in range(0, out_ref.shape[1], BAND):
        band = slice(at, at + BAND)
        phase = jnp.concatenate(
            [
                (k[:, band].astype(jnp.float32) + pair_ref[p, band].astype(jnp.float32))
                + f[:, band].astype(jnp.float32)
                for k, p, f in zip(keeps, pairs, fars)
            ],
            0,
        )
        turns = phase * (0.5 / math.pi)
        turns = turns - jnp.round(turns)
        square = turns * turns
        field = jnp.concatenate(
            [horner(COSINE, square), turns * horner(SINE, square)], 0
        ).astype(jnp.bfloat16)
        focal = jnp.dot(left_ref[...], field, preferred_element_type=jnp.float32)
        reals, imags = [], []
        for altitude in range(SLICES):
            real = focal[2 * SPOT * altitude : 2 * SPOT * altitude + SPOT]
            imag = focal[2 * SPOT * altitude + SPOT : 2 * SPOT * (altitude + 1)]
            cosine = column_ref[altitude : altitude + 1, band]
            sine = column_ref[SLICES + altitude : SLICES + altitude + 1, band]
            reals.append((real * cosine - imag * sine).astype(jnp.bfloat16))
            imags.append((real * sine + imag * cosine).astype(jnp.bfloat16))
        real = jnp.concatenate(reals, 0)
        imag = jnp.concatenate(imags, 0)
        for place in range(0, BAND, SUBPIX):
            spot = jnp.dot(
                jnp.concatenate([real[:, place : place + SUBPIX], imag[:, place : place + SUBPIX]], 1),
                right_ref[...],
                preferred_element_type=jnp.float32,
            )
            power = spot * spot
            power = power[:, :SPOT] + power[:, SPOT:]
            total = power[:SPOT]
            for altitude in range(1, SLICES):
                total = total + power[altitude * SPOT : (altitude + 1) * SPOT]
            to = slice(at + place, at + place + SUBPIX)
            lit = column_ref[2 * SLICES : 2 * SLICES + 1, to]
            out_ref[:, to] = (total * lit).astype(jnp.bfloat16)


def spots_of(left, right, column, keeps, pair, fars, start, width, whole):
    chunks = len(keeps)
    step = min(FINAL_COLS, width)
    at = start // step

    def part(array):
        skip = at if array.shape[1] == PCOLS else 0
        return pl.BlockSpec((array.shape[0], step), lambda i: (0, i + skip))

    taken = [column, *keeps, pair, *fars]
    grown = [] if whole is None else [whole]
    return pl.pallas_call(
        functools.partial(final_kernel, chunks, len(grown)),
        grid=(width // step,),
        out_shape=jax.ShapeDtypeStruct((SPOT, PCOLS), jnp.bfloat16),
        in_specs=[
            pl.BlockSpec(left.shape, lambda i: (0, 0)),
            pl.BlockSpec(right.shape, lambda i: (0, 0)),
            *map(part, taken),
            *(pl.BlockSpec(memory_space=pl.ANY) for _ in grown),
        ],
        out_specs=pl.BlockSpec((SPOT, step), lambda i: (0, i + at)),
        input_output_aliases={2 + len(taken): 0} if grown else {},
        compiler_params=pltpu.CompilerParams(vmem_limit_bytes=VMEM_LIMIT),
        cost_estimate=pl.CostEstimate(flops=1024, bytes_accessed=1024, transcendentals=0),
        name="spots",
    )(left, right, *taken, *grown)


def shards(layers, offsets, subap_valid, defocus, weights):
    index = lax.axis_index("dir").astype(jnp.int32)[None]
    tile = lax.axis_index("tile")
    total_rows = lax.axis_size("tile") * SUBPIX
    block = layers[0]
    own = [block[: CUTS[1]]]
    once = [shifted(own[0], -1)]

    real_part, imag_part, right = tables()
    row = (
        (tile * SUBPIX + jnp.arange(SUBPIX, dtype=jnp.int32)).astype(jnp.float32)
        - (total_rows - 1) / 2.0
    ) / SUBPIX
    col = (jnp.arange(PCOLS, dtype=jnp.float32) - (PCOLS - 1) / 2.0) / SUBPIX
    row_angle = defocus[:, None] * (row * row)[None, :]
    col_angle = defocus[:, None] * (col * col)[None, :]
    row_cos, row_sin = jnp.cos(row_angle)[:, None], jnp.sin(row_angle)[:, None]
    left_real = real_part[None] * row_cos - imag_part[None] * row_sin
    left_imag = real_part[None] * row_sin + imag_part[None] * row_cos
    left = jnp.concatenate(
        [
            jnp.concatenate([left_real, -left_imag], 2),
            jnp.concatenate([left_imag, left_real], 2),
        ],
        1,
    )
    left = left.reshape(SLICES * 2 * SPOT, 2 * SUBPIX).astype(jnp.bfloat16)
    share = jnp.sqrt(weights / jnp.sum(weights))[:, None]
    lit = jnp.repeat(subap_valid.astype(jnp.float32), SUBPIX, axis=1)
    column = jnp.concatenate([jnp.cos(col_angle) * share, jnp.sin(col_angle) * share, lit], 0)

    block = lax.optimization_barrier(block)
    own.append(block[CUTS[1] :])
    once.append(shifted(own[1], -1))
    once[0], offsets, column, left = lax.optimization_barrier((once[0], offsets, column, left))
    twice = [shifted(piece, -1) for piece in once]

    blocks = own + once + twice[:1]
    keep, send, cross, cross_send = terms(0, CUTS[1], index, offsets, blocks)
    joined = other_core(cross_send)
    joined, twice[1] = lax.optimization_barrier((joined, twice[1]))
    both = (send.astype(jnp.float32) + joined.astype(jnp.float32)).astype(jnp.bfloat16)
    keeps, fars = [keep], [other_chip(both)]

    blocks = own[1:] + once + twice
    keep, send, crosses = terms(CUTS[1], CUTS[2] - CUTS[1], index, offsets, blocks, (cross,))
    keeps.append(keep)
    pair = other_core(crosses)
    sides = []
    for a, b in zip(SIDES, SIDES[1:]):
        both = send[:, a:b].astype(jnp.float32) + pair[: send.shape[0], a:b].astype(jnp.float32)
        sides.append(other_chip(both.astype(jnp.bfloat16)))

    spots = None
    for side, a, b in zip(sides, SIDES, SIDES[1:]):
        spots = spots_of(left, right, column, keeps, pair, fars + [side], a, b - a, spots)
    return spots[None, None]


def solution(mesh):
    placed = (P("dir", "tile", None), P(), P("tile", None), P(), P())
    return jax.shard_map(
        shards, mesh=mesh, in_specs=placed, out_specs=P("dir", "tile", None, None), check_vma=False
    )
```
